32 devices in a mesh: tm: 2 (over x), space: 16 (over z, y, core).
Axes of the slice: x: 2, y: 2, z: 4, core: 2. Of those that a mesh axis runs over, the one named last changes fastest.
Arguments:
- flux: float32 [2, 65536], P('tm', 'space'), may hold values from -6 to 6
- noise: float32 [2, 65536], P('tm', 'space'), may hold values from -6 to 6
- prior_scale: float32 [65536], P('space'), may hold values from 0.3 to 3
- footprints: bfloat16 [2, 512, 32, 4096], P('tm', 'space'), may hold values from -0.09375 to 0.09375
- soundings: bfloat16 [2, 512, 32], P('tm', 'space'), may hold values from -6 to 6
- targets: int32 [2, 512, 1], P('tm', 'space'), may hold values from 0 to 15; in each aligned block of 32 rows (0 to 31, 32 to 63, ..., all dimensions but the last counted through in order) at most 4 rows name the same one
- basis: bfloat16 [65536, 256], P('space'), may hold values from -68 to 68
Outputs:
- proposal: float32 [2, 65536], P('tm', 'space')
- predicted: float32 [2, 512, 32], P('tm', 'space')
- info_factor: float32 [256, 256], replicated
- whitened_rhs: float32 [256], replicated
The draws below stay inside these ranges and needn't reach their ends.
Inputs may be any that keep to these rules, and one draw needn't show every extreme that they name: `targets`: in the rows of one device no tile is named more than 4 times, and in every draw some device names some tile exactly 4 times.
All inputs are finite; a program needn't handle non-finite values.
Results may differ from the reference program's by a relative error of at most 0.0047.
Values may be sent and summed in bfloat16 or wider, within the bound.
No kernel may reach another device: no remote copies, remote signals or barrier semaphores. Data moves between devices by JAX's collectives and lax.ppermute only.
A program may use at most 128 MiB of HBM per device.

```python
import math
import jax
import jax.numpy as jnp
import numpy as np
from jax import lax

PATCH = 64
REACH = 8
RANK = 256
OBS = 32
NB = 32
STEPS = 2
CAP = 4
TILE = 4096
CELLS = 65536
BLOCKS = 512
OBS_ALL = 32768
N_SPACE = 16


def draw_basis(key, part):
    keys = jax.random.split(key, 3)
    column_scale = jnp.exp(jax.random.uniform(keys[0], (RANK,), jnp.float32) * jnp.log(10.0))
    own_part = jnp.clip(jax.random.normal(keys[1], (CELLS, RANK), jnp.float32), -4.0, 4.0)
    shared_part = jnp.clip(jax.random.normal(keys[2], (CELLS, 16), jnp.float32), -4.0, 4.0)
    mixing = 0.7
    shared_full = jnp.tile(shared_part, (1, RANK // 16))
    return ((own_part + mixing * shared_full) * column_scale[None, :]).astype(jnp.bfloat16)


def block_scale(rng, shape, pieces, least, largest):
    gain = 1.0
    for dim, shards_of in pieces:
        steps = jax.random.uniform(jax.random.fold_in(jax.random.fold_in(rng, 6), dim), (shards_of,), jnp.float32, least / len(pieces), largest / len(pieces))
        gain = gain * jnp.repeat(jnp.exp(steps), shape[dim] // shards_of).reshape((-1,) + (1,) * (len(shape) - 1 - dim))
    return gain


def assign_block(stream_key, own, number, rows, number_of, top, bound, slope):
    sequence = jax.random.permutation(stream_key, number_of)
    heavy_load, ordinary = shares(number_of, rows * top, bound, slope, True), shares(number_of, rows * top, bound, slope, False)
    places = jnp.arange(number_of)

    def named(tallies, rotation):
        used = int((tallies > 0).sum())
        fixed = max(1, used // 4)
        moved = fixed + (places - fixed + rotation * (used - fixed)) % max(1, number_of - fixed)
        return jnp.zeros((number_of,), jnp.int32).at[sequence[jnp.where(places < fixed, places, moved)]].set(jnp.asarray(tallies, jnp.int32))

    tallies = jnp.where(number % 4 == 0, named(heavy_load, number // 4), named(ordinary, number - number // 4 - 1))
    mixed = jax.random.permutation(jax.random.fold_in(own, 3), number_of)
    donor, taker = mixed[0:number_of // 2 * 2:2], mixed[1:number_of // 2 * 2:2]
    room = jnp.minimum(tallies[donor] - 1, bound - tallies[taker]) // 2
    room = jnp.where((donor == sequence[0]) | (taker == sequence[0]) | (tallies[taker] == 0), 0, jnp.maximum(room, 0))
    moved = jax.random.randint(jax.random.fold_in(own, 4), (number_of // 2,), 0, 1 << 20) % (room + 1)
    tallies = tallies.at[donor].add(-moved).at[taker].add(moved)
    items = jnp.searchsorted(jnp.cumsum(tallies), jnp.arange(rows * top), side="right").astype(jnp.int32)
    listing = items.reshape(top, rows).T
    listing = listing[jax.random.permutation(jax.random.fold_in(own, 1), rows)]
    rotation = jax.random.randint(jax.random.fold_in(own, 2), (rows, 1), 0, top)
    return jnp.take_along_axis(listing, (jnp.arange(top)[None, :] + rotation) % top, axis=1)


def shares(count, total, bound, slope, full):
    portions = [(1 << 20) // math.isqrt(rank ** slope) + 1 for rank in range(1, count + 1)]
    largest = bound if full else min(bound, max(-(-total // count), total * portions[0] // sum(portions)))
    least = 1 if total - largest >= count - 1 else 0
    given, rest = [largest] + [least] * (count - 1), total - largest - least * (count - 1)
    while rest > 0:
        candidates = [i for i in range(1, count) if given[i] < largest] or [i for i in range(1, count) if given[i] < bound]
        pool, left = sum([portions[i] for i in candidates]), rest
        for i in candidates:
            extra = min(bound - given[i], max(1, left * portions[i] // pool), rest)
            given[i] = given[i] + extra
            rest = rest - extra
    return np.array(given)


def bell_draw(key, dims, spread, limit, cuts=(), kind=jnp.bfloat16):
    entries = jax.random.normal(key, dims, jnp.float32) * spread
    if len(cuts) > 0:
        entries = block_scale(key, dims, cuts, -0.22, 0.18) * entries
    return jnp.clip(entries, min=-limit, max=limit).astype(kind)


def setup_inputs(seed: int = 0) -> dict:
    arg_keys = jax.random.split(jax.random.key(seed), 8)
    flux = bell_draw(arg_keys[0], (STEPS, CELLS), 1.0, 6.0, ((0, 2), (1, 16)), jnp.float32)
    noise = bell_draw(arg_keys[1], (STEPS, CELLS), 1.0, 6.0, ((0, 2), (1, 16)), jnp.float32)
    prior_scale = jnp.clip(jnp.exp(math.log(3.0) - 2.3025851 * jax.random.uniform(arg_keys[2], (CELLS,), jnp.float32) ** block_scale(arg_keys[2], (CELLS,), ((0, 16),), -0.2, 0.2)), 0.3, 3.0)
    footprints = bell_draw(arg_keys[3], (STEPS, BLOCKS, OBS, TILE), TILE ** -0.5, 0.09375, ((0, 2), (1, 16)))
    soundings = bell_draw(arg_keys[4], (STEPS, BLOCKS, OBS), 1.0, 6.0, ((0, 2), (1, 16)))
    targets_keys = jax.random.split(jax.random.fold_in(arg_keys[5], 1), STEPS * BLOCKS // NB)
    targets_turns = jax.random.permutation(jax.random.fold_in(arg_keys[5], 3), STEPS * BLOCKS // NB)
    targets = jax.vmap(lambda own, number: assign_block(jax.random.fold_in(arg_keys[5], 2), own, number, NB, N_SPACE, 1, CAP, 2))(targets_keys, targets_turns).reshape((STEPS, BLOCKS, 1))
    basis = draw_basis(jax.random.fold_in(arg_keys[7], 71), 0)
    return dict(flux=flux, noise=noise, prior_scale=prior_scale, footprints=footprints, soundings=soundings, targets=targets, basis=basis)


BETA = 0.6
KEEP = 0.8

def kernel_weights(reach):
    offsets = jnp.abs(jnp.arange(-reach, reach + 1).astype(jnp.float32))
    profile = (1.0 + 2.0 * offsets / reach) * jnp.exp(-2.0 * offsets / reach)
    return profile / jnp.sqrt(jnp.sum(profile * profile))

def reference(flux, noise, prior_scale, footprints, soundings, targets, basis):
    weights = kernel_weights(REACH)
    grid_rows = N_SPACE * PATCH
    grid = noise.reshape(STEPS, grid_rows, PATCH)
    padded = jnp.pad(grid, ((0, 0), (REACH, REACH), (0, 0)))
    along_rows = jnp.zeros_like(grid)
    for position in range(2 * REACH + 1):
        along_rows = along_rows + weights[position] * padded[:, position:position + grid_rows, :]
    smooth = jnp.zeros_like(grid)
    for position in range(2 * REACH + 1):
        smooth = smooth + weights[position] * jnp.roll(along_rows, REACH - position, axis=2)
    proposal = KEEP * flux + BETA * prior_scale[None, :] * smooth.reshape(STEPS, CELLS)
    tiles_half = proposal.astype(jnp.bfloat16).reshape(STEPS, N_SPACE, TILE)
    basis_tiles = basis.reshape(N_SPACE, TILE, RANK)
    jac_scale = float(OBS_ALL) ** (-0.5)

    def one_block(carry, block_item):
        gram_sum, projected = carry
        footprint, observed, step_id, target = block_item
        tile_values = tiles_half[step_id, target]
        tile_basis = basis_tiles[target]
        predicted_row = jnp.dot(footprint.astype(jnp.float32), tile_values.astype(jnp.float32), preferred_element_type=jnp.float32)
        jacobian = (jnp.dot(footprint.astype(jnp.float32), tile_basis.astype(jnp.float32), preferred_element_type=jnp.float32) * jac_scale).astype(jnp.bfloat16)
        misfit = observed.astype(jnp.float32) - predicted_row
        gram_sum = gram_sum + jnp.dot(jacobian.T.astype(jnp.float32), jacobian.astype(jnp.float32), preferred_element_type=jnp.float32)
        projected = projected + jnp.dot(jacobian.astype(jnp.float32).T, misfit, precision=lax.Precision.HIGHEST)
        return ((gram_sum, projected), predicted_row)
    step_ids = jnp.broadcast_to(jnp.arange(STEPS, dtype=jnp.int32)[:, None], (STEPS, BLOCKS)).reshape(-1)
    block_items = (footprints.reshape(STEPS * BLOCKS, OBS, TILE), soundings.reshape(STEPS * BLOCKS, OBS), step_ids, targets.reshape(-1).astype(jnp.int32))
    start_carry = (jnp.zeros((RANK, RANK), jnp.float32), jnp.zeros((RANK,), jnp.float32))
    (gram_sum, projected), predicted = lax.scan(one_block, start_carry, block_items)
    information = jnp.eye(RANK, dtype=jnp.float32) + gram_sum
    factor_low = jnp.linalg.cholesky(information)
    whitened_rhs = jax.scipy.linalg.solve_triangular(factor_low, projected, lower=True)
    return (proposal, predicted.reshape(STEPS, BLOCKS, OBS), factor_low.T, whitened_rhs)
```

```python
import jax
import jax.numpy as jnp
from jax import lax
from jax.experimental import pallas as pl
from jax.experimental.pallas import tpu as pltpu
from jax.sharding import PartitionSpec as P

PATCH = 64
REACH = 8


BETA = 0.6
KEEP = 0.8
HIGHEST = lax.Precision.HIGHEST


def padded(shard, sides, width):
    for axis, dim in sides:
        devices, length = (lax.axis_size(axis), shard.shape[dim])
        up = [(i, (i + 1) % devices) for i in range(devices - 1)]
        down = [(j, i) for i, j in up]
        last = lax.slice_in_dim(shard, length - width, length, axis=dim)
        leading = lax.slice_in_dim(shard, 0, width, axis=dim)
        before = lax.ppermute(last, axis, up)
        after = lax.ppermute(leading, axis, down)
        shard = jnp.concatenate([before, shard, after], axis=dim)
    return shard


def kernel_weights(reach):
    offsets = jnp.abs(jnp.arange(-reach, reach + 1).astype(jnp.float32))
    profile = (1.0 + 2.0 * offsets / reach) * jnp.exp(-2.0 * offsets / reach)
    return profile / jnp.sqrt(jnp.sum(profile * profile))


def make_proposal(flux, noise, prior_scale):
    patch_edge = PATCH
    cell_count = flux.shape[1]
    weights = kernel_weights(REACH)
    extended = padded(noise, (("space", 1),), REACH * patch_edge)
    extended_grid = extended.reshape(patch_edge + 2 * REACH, patch_edge)
    row_offset = jnp.arange(patch_edge + 2 * REACH)[None, :] - jnp.arange(patch_edge)[:, None]
    col_offset = (
        jnp.arange(patch_edge)[:, None] - jnp.arange(patch_edge)[None, :] + REACH
    ) % patch_edge
    row_band = jnp.zeros((patch_edge, patch_edge + 2 * REACH), jnp.float32)
    col_circulant = jnp.zeros((patch_edge, patch_edge), jnp.float32)
    for position in range(2 * REACH + 1):
        row_band = row_band + weights[position] * (row_offset == position).astype(jnp.float32)
        col_circulant = col_circulant + weights[position] * (col_offset == position).astype(
            jnp.float32
        )
    along_rows = jnp.dot(row_band, extended_grid, precision=HIGHEST)
    smooth = jnp.dot(along_rows, col_circulant, precision=HIGHEST)
    return KEEP * flux + BETA * prior_scale[None, :] * smooth.reshape(1, cell_count)


def slots_of(destination, tile_ids, capacity):
    match = destination[None, :] == tile_ids[:, None]
    rank = jnp.cumsum(match.astype(jnp.int32), axis=1) - 1
    block = jnp.arange(destination.shape[0], dtype=jnp.int32)
    taken = match[:, None, :] & (rank[:, None, :] == jnp.arange(capacity)[None, :, None])
    slots = jnp.sum(jnp.where(taken, block[None, None, :], 0), axis=2)
    return slots.reshape(-1).astype(jnp.int32), jnp.sum(match, axis=1).astype(jnp.int32)


def block_products(slots, counts, starts, footprints, tiles, windows, out_dtype):
    blocks, rows, _ = footprints.shape
    tile_count, piece_count = len(tiles), len(tiles[0])
    rank = tiles[0][0].shape[1]
    capacity = slots.shape[0] // tile_count
    depth = sum(windows)
    places = [sum(windows[:p]) for p in range(piece_count)]

    def kernel(slots_ref, counts_ref, starts_ref, f_ref, *rest):
        piece_refs = rest[: tile_count * piece_count]
        out_ref, f_v, b_v, f_sem, b_sem = rest[tile_count * piece_count :]
        f_copies = []
        for p in range(piece_count):
            begin = pl.multiple_of(starts_ref[p], 128)
            copy = pltpu.make_async_copy(
                f_ref.at[:, :, pl.ds(begin, windows[p])],
                f_v.at[:, :, pl.ds(places[p], windows[p])],
                f_sem.at[p],
            )
            f_copies.append(copy)
        for s in range(tile_count):
            for p in range(piece_count):
                pltpu.make_async_copy(
                    piece_refs[s * piece_count + p],
                    b_v.at[s, pl.ds(places[p], windows[p])],
                    b_sem.at[s, p],
                ).start()
            if s == 0:
                for copy in f_copies:
                    copy.start()
        for copy in f_copies:
            copy.wait()

        def step(s, carry):
            for p in range(piece_count):
                pltpu.make_async_copy(
                    piece_refs[p], b_v.at[s, pl.ds(places[p], windows[p])], b_sem.at[s, p]
                ).wait()
            lhs = jnp.concatenate(
                [f_v[slots_ref[s * capacity + j]] for j in range(capacity)], axis=0
            )
            product = jnp.dot(lhs, b_v[s], preferred_element_type=jnp.float32)
            for j in range(capacity):

                @pl.when(counts_ref[s] > j)
                def _():
                    at = pl.multiple_of(slots_ref[s * capacity + j] * rows, rows)
                    out_ref[pl.ds(at, rows), :] = product[j * rows : (j + 1) * rows].astype(
                        out_dtype
                    )

            return carry

        lax.fori_loop(0, tile_count, step, 0)

    flat = [piece for tile in tiles for piece in tile]
    smem = pl.BlockSpec(memory_space=pltpu.SMEM)
    hbm = pl.BlockSpec(memory_space=pl.ANY)
    return pl.pallas_call(
        kernel,
        out_shape=jax.ShapeDtypeStruct((blocks * rows, rank), out_dtype),
        in_specs=[smem, smem, smem, hbm] + [hbm] * len(flat),
        out_specs=pl.BlockSpec(memory_space=pltpu.VMEM),
        scratch_shapes=[
            pltpu.VMEM((blocks, rows, depth), jnp.bfloat16),
            pltpu.VMEM((tile_count, depth, rank), jnp.bfloat16),
            pltpu.SemaphoreType.DMA((piece_count,)),
            pltpu.SemaphoreType.DMA((tile_count, piece_count)),
        ],
        compiler_params=pltpu.CompilerParams(vmem_limit_bytes=56 * 2**20),
        cost_estimate=pl.CostEstimate(
            flops=2 * tile_count * capacity * rows * depth * rank,
            bytes_accessed=2 * depth * (tile_count * rank + blocks * rows),
            transcendentals=0,
        ),
    )(slots, counts, starts, footprints, *flat)


def information_sums(own, received, misfit, scale):
    rows, rank = own.shape
    half = rank // 2
    packed = half + half // 2 + 16

    def kernel(own_ref, received_ref, misfit_ref, out_ref):
        jacobian = (own_ref[...] + received_ref[...].astype(jnp.float32)) * scale
        jacobian = jacobian.astype(jnp.bfloat16)
        gram = lax.dot_general(
            jacobian, jacobian, (((0,), (0,)), ((), ())), preferred_element_type=jnp.float32
        )
        out_ref[0:half, :] = gram[0:half, :]
        out_ref[half : half + half // 2, 0:half] = gram[half : half + half // 2, half:]
        out_ref[half : half + half // 2, half:] = gram[half + half // 2 :, half:]
        rest = misfit_ref[...]
        parts = []
        for _ in range(3):
            part = rest.astype(jnp.bfloat16)
            parts.append(part)
            rest = rest - part.astype(jnp.float32)
        lhs = jnp.concatenate(parts + [jnp.zeros((16 - 3, rows), jnp.bfloat16)], axis=0)
        projected = jnp.dot(lhs, jacobian, preferred_element_type=jnp.float32)
        total = projected[0:1] + projected[1:2] + projected[2:3]
        out_ref[half + half // 2 :, :] = jnp.broadcast_to(total, (16, rank))

    return pl.pallas_call(
        kernel,
        out_shape=jax.ShapeDtypeStruct((packed, rank), jnp.float32),
        compiler_params=pltpu.CompilerParams(vmem_limit_bytes=32 * 2**20),
    )(own, received, misfit)


def finish_factor(packed):
    rank = packed.shape[1]
    half = rank // 2
    quarter = half // 2
    wide = rank + 128
    strip = 64

    def kernel(in_ref, up_ref, rhs_ref, work, factor):
        top = in_ref[0:half, :]
        work[0:half, 0:rank] = top
        work[half:, 0:half] = top[:, half:].T
        work[half : half + quarter, half:rank] = in_ref[half : half + quarter, 0:half]
        work[half + quarter :, half:rank] = in_ref[half : half + quarter, half:]
        for k in range(0, rank, 128):
            row = lax.broadcasted_iota(jnp.int32, (128, 128), 0)
            col = lax.broadcasted_iota(jnp.int32, (128, 128), 1)
            work[k : k + 128, k : k + 128] += (row == col).astype(jnp.float32)
        column = in_ref[half + quarter : half + quarter + 8, :].T
        work[:, rank:] = jnp.broadcast_to(column[:, 0:1], (rank, 128))

        sub = lax.broadcasted_iota(jnp.int32, (8, wide), 0)
        for base in range(0, rank, strip):
            skip = base // 128 * 128
            width = wide - skip
            sub_w = sub[:, skip:]
            tiles = [work[base + 8 * i : base + 8 * i + 8, skip:] for i in range(strip // 8)]
            for p in range(strip // 8):
                at = base + 8 * p - skip
                r = [jnp.broadcast_to(tiles[p][j : j + 1, :], (8, width)) for j in range(8)]
                d = {}
                for j in range(8):
                    for m in range(j, 8):
                        d[j, m] = jnp.broadcast_to(r[j][:, at + m : at + m + 1], (8, 128))
                inv, e = [], {}
                for j in range(8):
                    inv.append(lax.rsqrt(d[j, j]))
                    for m in range(j + 1, 8):
                        e[j, m] = d[j, m] * inv[j]
                    for l in range(j + 1, 8):
                        for m in range(l, 8):
                            d[l, m] = d[l, m] - e[j, l] * e[j, m]
                lanes = lambda x: jnp.concatenate([x] * (width // 128), axis=1)
                u = []
                for j in range(8):
                    u.append(r[j] * lanes(inv[j]))
                    for l in range(j + 1, 8):
                        r[l] = r[l] - lanes(e[j, l]) * u[j]
                whole = jnp.zeros((8, width), jnp.float32)
                for j in range(8):
                    whole = jnp.where(sub_w == j, u[j], whole)
                factor[base + 8 * p : base + 8 * p + 8, skip:] = whole
                for i in range(p + 1, strip // 8):
                    a = [
                        jnp.broadcast_to(tiles[i][:, at + j : at + j + 1], (8, 128))
                        for j in range(8)
                    ]
                    tile = tiles[i]
                    for j in range(8):
                        m_j = a[j] * inv[j]
                        for l in range(j + 1, 8):
                            a[l] = a[l] - m_j * e[j, l]
                        tile = tile - lanes(m_j) * u[j]
                    tiles[i] = tile
            low = base + strip
            if low < rank:
                keep = low // 128 * 128
                left = factor[base:low, low:rank]
                right = factor[base:low, keep:]
                work[low:, keep:] -= lax.dot_general(
                    left,
                    right,
                    (((0,), (0,)), ((), ())),
                    precision=HIGHEST,
                    preferred_element_type=jnp.float32,
                )
        for k in range(0, rank, 128):
            for c in range(0, rank, 128):
                if c < k:
                    up_ref[k : k + 128, c : c + 128] = jnp.zeros((128, 128), jnp.float32)
                elif c > k:
                    up_ref[k : k + 128, c : c + 128] = factor[k : k + 128, c : c + 128]
                else:
                    row = lax.broadcasted_iota(jnp.int32, (128, 128), 0)
                    col = lax.broadcasted_iota(jnp.int32, (128, 128), 1)
                    up_ref[k : k + 128, c : c + 128] = jnp.where(
                        col >= row, factor[k : k + 128, c : c + 128], 0.0
                    )
            rhs_ref[:, k : k + 128] = factor[k : k + 128, rank:].T[0:8, :]

    return pl.pallas_call(
        kernel,
        out_shape=(
            jax.ShapeDtypeStruct((rank, rank), jnp.float32),
            jax.ShapeDtypeStruct((8, rank), jnp.float32),
        ),
        scratch_shapes=[
            pltpu.VMEM((rank, wide), jnp.float32),
            pltpu.VMEM((rank, wide), jnp.float32),
        ],
        compiler_params=pltpu.CompilerParams(vmem_limit_bytes=32 * 2**20),
    )(packed)


def per_device(flux, noise, prior_scale, footprints, soundings, targets, basis):
    tile_count = lax.axis_size("space")
    step_count = lax.axis_size("tm")
    _, block_count, obs_count, cell_count = footprints.shape
    rank = basis.shape[1]
    capacity = max(2, (2 * block_count + tile_count - 1) // tile_count)
    place = lax.axis_index("space")
    top = tile_count // 4
    side = lax.axis_index("tm") % 2
    share = cell_count // 2

    over_last = [(i, i ^ 1) for i in range(tile_count)]
    over_mid = [(i, i ^ 2) for i in range(tile_count)]
    over_top = [(i, (i - 4) % tile_count) for i in range(tile_count)]
    over_step = [(i, i ^ 1) for i in range(step_count)]

    own_blocks = footprints[0]
    theirs = lax.dynamic_slice_in_dim(own_blocks, (1 - side) * share, share, axis=2)
    swapped = lax.ppermute(theirs, "tm", over_step)
    destination = targets[0, :, 0]
    other_destination = lax.ppermute(destination, "tm", over_step)

    cut = share // 2
    own_half = lax.dynamic_slice_in_dim(basis, side * share, share, axis=0)
    pieces = [own_half[:cut], own_half[cut:]]
    near = [pieces]
    for k in range(1, top):
        near.append([lax.ppermute(piece, "space", over_top) for piece in near[k - 1]])
    far = []
    for k in range(top):
        row = []
        for p in range(2):
            if k == top - 1 and p == 0 and k > 0:
                row.append(lax.ppermute(far[k - 1][p], "space", over_top))
            else:
                row.append(lax.ppermute(near[k][p], "space", over_mid))
        far.append(row)
    tiles, tile_ids = [], []
    for k in range(top):
        at = (place + 4 * k) % tile_count
        for held, index in ((near[k], at), (far[k], at ^ 2)):
            tiles.append(held)
            tile_ids.append(index)
            tiles.append([lax.ppermute(piece, "space", over_last) for piece in held])
            tile_ids.append(index ^ 1)
    tile_ids = jnp.stack(tile_ids)

    proposal = make_proposal(flux, noise, prior_scale)
    halves = lax.all_gather(proposal.astype(jnp.bfloat16), "space", axis=0, tiled=True)
    every = lax.dot_general(
        halves,
        own_blocks.reshape(block_count * obs_count, cell_count),
        (((1,), (1,)), ((), ())),
        preferred_element_type=jnp.float32,
    )
    named = jnp.arange(tile_count)[:, None] == jnp.repeat(destination, obs_count)[None, :]
    predicted = jnp.sum(jnp.where(named, every, 0.0), axis=0, keepdims=True)
    misfit = soundings.reshape(1, -1).astype(jnp.float32) - predicted

    slots, counts = slots_of(destination, tile_ids, capacity)
    other_slots, other_counts = slots_of(other_destination, tile_ids, capacity)
    windows = [cut, share - cut]
    start = (side * share).astype(jnp.int32)
    starts = jnp.stack([start, start + cut])
    others = block_products(
        other_slots,
        other_counts,
        jnp.array([0, cut], jnp.int32),
        swapped,
        tiles,
        windows,
        jnp.bfloat16,
    )
    received = lax.ppermute(others, "tm", over_step)
    own = block_products(slots, counts, starts, own_blocks, tiles, windows, jnp.float32)
    jac_scale = float(step_count * tile_count * block_count * obs_count) ** (-0.5)
    total = information_sums(own, received, misfit, jac_scale)

    half = total.shape[0] // 2
    last = place % 2
    mine = lax.dynamic_slice_in_dim(total, last * half, half, axis=0)
    sent = lax.dynamic_slice_in_dim(total, (1 - last) * half, half, axis=0)
    mine = mine + lax.ppermute(sent, "space", over_last)
    shift = 1
    while shift < step_count:
        pairs = [(i, i ^ shift) for i in range(step_count)]
        mine = mine + lax.ppermute(mine, "tm", pairs)
        shift *= 2
    shift = 2
    while shift < tile_count:
        pairs = [(i, i ^ shift) for i in range(tile_count)]
        mine = mine + lax.ppermute(mine, "space", pairs)
        shift *= 2
    back = lax.ppermute(mine, "space", over_last)
    packed = jnp.where(
        last == 0, jnp.concatenate([mine, back]), jnp.concatenate([back, mine])
    )
    factor_up, rhs = finish_factor(packed)
    return (
        proposal,
        predicted.reshape(1, block_count, obs_count),
        factor_up,
        rhs[0],
    )


def solution(mesh):
    return jax.shard_map(
        per_device,
        mesh=mesh,
        in_specs=(
            P("tm", "space"),
            P("tm", "space"),
            P("space"),
            P("tm", "space", None, None),
            P("tm", "space", None),
            P("tm", "space", None),
            P("space", None),
        ),
        out_specs=(P("tm", "space"), P("tm", "space", None), P(), P()),
        check_vma=False,
    )
```

```python
import jax
import jax.numpy as jnp
import numpy as np
from jax import lax
from jax.experimental import pallas as pl
from jax.experimental.pallas import tpu as pltpu
from jax.sharding import PartitionSpec as P

PATCH = 64
REACH = 8


BETA = 0.6
KEEP = 0.8
HIGHEST = lax.Precision.HIGHEST


def kernel_weights(reach):
    offsets = np.abs(np.arange(-reach, reach + 1)).astype(np.float32)
    profile = (1.0 + 2.0 * offsets / reach) * np.exp(-2.0 * offsets / reach)
    return [float(w) for w in profile / np.sqrt(np.sum(profile * profile))]


def make_proposal(flux, noise, prior_scale):
    edge = PATCH
    cells = flux.shape[1]
    width = REACH * edge
    weights = kernel_weights(REACH)
    devices = lax.axis_size("space")
    up = [(i, (i + 1) % devices) for i in range(devices - 1)]
    down = [(j, i) for i, j in up]
    before = lax.ppermute(noise[:, cells - width :], "space", up)
    after = lax.ppermute(noise[:, :width], "space", down)
    extended = jnp.concatenate([before, noise, after], axis=1).reshape(edge + 2 * REACH, edge)

    def kernel(extended_ref, flux_ref, scale_ref, out_ref):
        rows = jnp.zeros((edge, edge), jnp.float32)
        for position in range(2 * REACH + 1):
            rows = rows + weights[position] * extended_ref[position : position + edge, :]
        twice = jnp.concatenate([rows, rows], axis=1)
        smooth = jnp.zeros((edge, 2 * edge), jnp.float32)
        for position in range(2 * REACH + 1):
            shift = (REACH - position) % (2 * edge)
            rolled = pltpu.roll(twice, shift, 1) if shift else twice
            smooth = smooth + weights[position] * rolled
        out_ref[...] = KEEP * flux_ref[...] + BETA * scale_ref[...] * smooth[:, :edge]

    proposal = pl.pallas_call(
        kernel, out_shape=jax.ShapeDtypeStruct((edge, edge), jnp.float32)
    )(extended, flux.reshape(edge, edge), prior_scale.reshape(edge, edge))
    flat = proposal.reshape(1, cells)
    return flat, flat.astype(jnp.bfloat16), (before, after)


def slots_of(destination, tile_ids, capacity):
    match = destination[None, :] == tile_ids[:, None]
    rank = jnp.cumsum(match.astype(jnp.int32), axis=1) - 1
    block = jnp.arange(destination.shape[0], dtype=jnp.int32)
    taken = match[:, None, :] & (rank[:, None, :] == jnp.arange(capacity)[None, :, None])
    slots = jnp.sum(jnp.where(taken, block[None, None, :], 0), axis=2)
    return slots.reshape(-1).astype(jnp.int32), jnp.sum(match, axis=1).astype(jnp.int32)


def block_products(slots, counts, sources, tiles, jobs, capacity, out_dtype, base=None):
    blocks, rows, _ = sources[0][0].shape
    rank = tiles[0][0][0].shape[1]
    widths = [width for _, _, width in sources]
    places = [sum(widths[:i]) for i in range(len(widths))]
    depth = max(high - low for _, low, high in jobs)
    arrays, copies = [], []
    for s, low, high in jobs:
        parts, at = [], 0
        for array, first, count in tiles[s]:
            begin, end = max(low, at), min(high, at + count)
            if begin < end:
                known = [i for i, other in enumerate(arrays) if other is array]
                if not known:
                    arrays.append(array)
                    known = [len(arrays) - 1]
                parts.append((known[0], first + begin - at, begin - low, end - begin))
            at += count
        copies.append(parts)
    most = max(len(parts) for parts in copies)
    ahead = min(4, len(jobs))

    def kernel(slots_ref, counts_ref, starts_ref, *rest):
        f_refs, rest = rest[: len(sources)], rest[len(sources) :]
        b_refs, rest = rest[: len(arrays)], rest[len(arrays) :]
        if base is not None:
            base_ref, rest = rest[0], rest[1:]
        out_ref, f_v, b_v, f_sem, b_sem = rest
        f_copies = []
        for i, width in enumerate(widths):
            begin = pl.multiple_of(starts_ref[i], 128)
            copy = pltpu.make_async_copy(
                f_refs[i].at[:, :, pl.ds(begin, width)],
                f_v.at[:, :, pl.ds(places[i], width)],
                f_sem.at[i],
            )
            copy.start()
            f_copies.append(copy)

        def job_copies(n):
            return [
                pltpu.make_async_copy(
                    b_refs[i].at[pl.ds(first, count)],
                    b_v.at[n, pl.ds(place, count)],
                    b_sem.at[n, part],
                )
                for part, (i, first, place, count) in enumerate(copies[n])
            ]

        for n in range(ahead):
            for copy in job_copies(n):
                copy.start()
        if base is not None and out_dtype == jnp.float32:
            out_ref[...] = base_ref[...]
        for copy in f_copies:
            copy.wait()
        for n, (s, low, high) in enumerate(jobs):
            if n + ahead < len(jobs):
                for copy in job_copies(n + ahead):
                    copy.start()
            for copy in job_copies(n):
                copy.wait()
            lhs = jnp.concatenate(
                [f_v[slots_ref[s * capacity + j], :, low:high] for j in range(capacity)], axis=0
            )
            product = jnp.dot(
                lhs, b_v[n, 0 : high - low, :], preferred_element_type=jnp.float32
            )
            for j in range(capacity):

                @pl.when(counts_ref[s] > j)
                def _():
                    at = pl.multiple_of(slots_ref[s * capacity + j] * rows, rows)
                    part = product[j * rows : (j + 1) * rows]
                    if low > 0:
                        part = part + base_ref[pl.ds(at, rows), :]
                    out_ref[pl.ds(at, rows), :] = part.astype(out_dtype)

    smem = pl.BlockSpec(memory_space=pltpu.SMEM)
    vmem = pl.BlockSpec(memory_space=pltpu.VMEM)
    hbm = pl.BlockSpec(memory_space=pl.ANY)
    extra = [] if base is None else [base]
    starts = jnp.stack([jnp.asarray(first, jnp.int32) for _, first, _ in sources])
    cells = sum(high - low for _, low, high in jobs)
    return pl.pallas_call(
        kernel,
        out_shape=jax.ShapeDtypeStruct((blocks * rows, rank), out_dtype),
        in_specs=[smem] * 3 + [hbm] * (len(sources) + len(arrays)) + [vmem] * len(extra),
        out_specs=vmem,
        scratch_shapes=[
            pltpu.VMEM((blocks, rows, sum(widths)), jnp.bfloat16),
            pltpu.VMEM((len(jobs), depth, rank), jnp.bfloat16),
            pltpu.SemaphoreType.DMA((len(sources),)),
            pltpu.SemaphoreType.DMA((len(jobs), most)),
        ],
        compiler_params=pltpu.CompilerParams(vmem_limit_bytes=56 * 2**20),
        cost_estimate=pl.CostEstimate(
            flops=2 * cells * capacity * rows * rank,
            bytes_accessed=2 * cells * rank + 2 * blocks * rows * sum(widths),
            transcendentals=0,
        ),
    )(slots, counts, starts, *[f for f, _, _ in sources], *arrays, *extra)


def information_sums(own, received, misfit, scale):
    rows, rank = own.shape
    half = rank // 2
    packed = half + half // 2 + 16

    def kernel(own_ref, received_ref, misfit_ref, out_ref):
        jacobian = (own_ref[...] + received_ref[...].astype(jnp.float32)) * scale
        jacobian = jacobian.astype(jnp.bfloat16)
        gram = lax.dot_general(
            jacobian, jacobian, (((0,), (0,)), ((), ())), preferred_element_type=jnp.float32
        )
        out_ref[0:half, :] = gram[0:half, :]
        out_ref[half : half + half // 2, 0:half] = gram[half : half + half // 2, half:]
        out_ref[half : half + half // 2, half:] = gram[half + half // 2 :, half:]
        rest = misfit_ref[...]
        parts = []
        for _ in range(3):
            part = rest.astype(jnp.bfloat16)
            parts.append(part)
            rest = rest - part.astype(jnp.float32)
        lhs = jnp.concatenate(parts + [jnp.zeros((16 - 3, rows), jnp.bfloat16)], axis=0)
        projected = jnp.dot(lhs, jacobian, preferred_element_type=jnp.float32)
        total = projected[0:1] + projected[1:2] + projected[2:3]
        out_ref[half + half // 2 :, :] = jnp.broadcast_to(total, (16, rank))

    return pl.pallas_call(
        kernel,
        out_shape=jax.ShapeDtypeStruct((packed, rank), jnp.float32),
        compiler_params=pltpu.CompilerParams(vmem_limit_bytes=32 * 2**20),
    )(own, received, misfit)


def finish_factor(packed):
    rank = packed.shape[1]
    half = rank // 2
    quarter = half // 2
    wide = rank + 128
    strip = 64

    def kernel(in_ref, up_ref, rhs_ref, work, factor):
        top = in_ref[0:half, :]
        work[0:half, 0:rank] = top
        work[half:, 0:half] = top[:, half:].T
        work[half : half + quarter, half:rank] = in_ref[half : half + quarter, 0:half]
        work[half + quarter :, half:rank] = in_ref[half : half + quarter, half:]
        for k in range(0, rank, 128):
            row = lax.broadcasted_iota(jnp.int32, (128, 128), 0)
            col = lax.broadcasted_iota(jnp.int32, (128, 128), 1)
            work[k : k + 128, k : k + 128] += (row == col).astype(jnp.float32)
        column = in_ref[half + quarter : half + quarter + 8, :].T
        work[:, rank:] = jnp.broadcast_to(column[:, 0:1], (rank, 128))

        sub = lax.broadcasted_iota(jnp.int32, (8, wide), 0)
        for base in range(0, rank, strip):
            skip = base // 128 * 128
            width = wide - skip
            sub_w = sub[:, skip:]
            tiles = [work[base + 8 * i : base + 8 * i + 8, skip:] for i in range(strip // 8)]
            for p in range(strip // 8):
                at = base + 8 * p - skip
                r = [jnp.broadcast_to(tiles[p][j : j + 1, :], (8, width)) for j in range(8)]
                d = {}
                for j in range(8):
                    for m in range(j, 8):
                        d[j, m] = jnp.broadcast_to(r[j][:, at + m : at + m + 1], (8, 128))
                inv, e = [], {}
                for j in range(8):
                    inv.append(lax.rsqrt(d[j, j]))
                    for m in range(j + 1, 8):
                        e[j, m] = d[j, m] * inv[j]
                    for l in range(j + 1, 8):
                        for m in range(l, 8):
                            d[l, m] = d[l, m] - e[j, l] * e[j, m]
                lanes = lambda x: jnp.concatenate([x] * (width // 128), axis=1)
                u = []
                for j in range(8):
                    u.append(r[j] * lanes(inv[j]))
                    for l in range(j + 1, 8):
                        r[l] = r[l] - lanes(e[j, l]) * u[j]
                whole = jnp.zeros((8, width), jnp.float32)
                for j in range(8):
                    whole = jnp.where(sub_w == j, u[j], whole)
                factor[base + 8 * p : base + 8 * p + 8, skip:] = whole
                for i in range(p + 1, strip // 8):
                    a = [
                        jnp.broadcast_to(tiles[i][:, at + j : at + j + 1], (8, 128))
                        for j in range(8)
                    ]
                    tile = tiles[i]
                    for j in range(8):
                        m_j = a[j] * inv[j]
                        for l in range(j + 1, 8):
                            a[l] = a[l] - m_j * e[j, l]
                        tile = tile - lanes(m_j) * u[j]
                    tiles[i] = tile
            low = base + strip
            if low < rank:
                keep = low // 128 * 128
                left = factor[base:low, low:rank]
                right = factor[base:low, keep:]
                work[low:, keep:] -= lax.dot_general(
                    left,
                    right,
                    (((0,), (0,)), ((), ())),
                    precision=HIGHEST,
                    preferred_element_type=jnp.float32,
                )
        for k in range(0, rank, 128):
            for c in range(0, rank, 128):
                if c < k:
                    up_ref[k : k + 128, c : c + 128] = jnp.zeros((128, 128), jnp.float32)
                elif c > k:
                    up_ref[k : k + 128, c : c + 128] = factor[k : k + 128, c : c + 128]
                else:
                    row = lax.broadcasted_iota(jnp.int32, (128, 128), 0)
                    col = lax.broadcasted_iota(jnp.int32, (128, 128), 1)
                    up_ref[k : k + 128, c : c + 128] = jnp.where(
                        col >= row, factor[k : k + 128, c : c + 128], 0.0
                    )
            rhs_ref[:, k : k + 128] = factor[k : k + 128, rank:].T[0:8, :]

    return pl.pallas_call(
        kernel,
        out_shape=(
            jax.ShapeDtypeStruct((rank, rank), jnp.float32),
            jax.ShapeDtypeStruct((8, rank), jnp.float32),
        ),
        scratch_shapes=[
            pltpu.VMEM((rank, wide), jnp.float32),
            pltpu.VMEM((rank, wide), jnp.float32),
        ],
        compiler_params=pltpu.CompilerParams(vmem_limit_bytes=32 * 2**20),
    )(packed)


def per_device(flux, noise, prior_scale, footprints, soundings, targets, basis):
    tile_count = lax.axis_size("space")
    step_count = lax.axis_size("tm")
    _, block_count, obs_count, cell_count = footprints.shape
    rank = basis.shape[1]
    capacity = max(2, (2 * block_count + tile_count - 1) // tile_count)
    place = lax.axis_index("space")
    top = tile_count // 4
    side = lax.axis_index("tm") % 2
    share = cell_count // 2

    over_last = [(i, i ^ 1) for i in range(tile_count)]
    over_mid = [(i, i ^ 2) for i in range(tile_count)]
    over_top = [(i, (i - 4) % tile_count) for i in range(tile_count)]
    over_step = [(i, i ^ 1) for i in range(step_count)]

    destination = targets[0, :, 0]
    other_destination = lax.ppermute(destination, "tm", over_step)
    proposal, rounded, rims = make_proposal(flux, noise, prior_scale)

    own_blocks = footprints[0]
    begin = (1 - side) * share
    to_send = lax.dynamic_slice_in_dim(own_blocks, begin, share, axis=2)
    to_send, other_destination = lax.optimization_barrier((to_send, other_destination))
    swapped = lax.ppermute(to_send, "tm", over_step)

    basis, _, _ = lax.optimization_barrier((basis, rims, to_send))
    own_half = lax.dynamic_slice_in_dim(basis, side * share, share, axis=0)
    cut = share // 2
    first = own_half[:cut]
    second = jnp.concatenate([own_half[cut:], rounded.reshape(-1, rank)], axis=0)

    def forward(x):
        return lax.ppermute(x, "space", over_last)

    def both(way):
        return jnp.concatenate([lax.ppermute(x, "space", way) for x in (first, second)], axis=0)

    whole = [(0, share)]
    near = [[(first, 0, cut), (second, 0, share - cut)]]
    near_array, far_array = both(over_top), both(over_mid)
    far = [[(far_array, 0, share)]]
    tail = share + cell_count // rank
    for k in range(1, top):
        if k > 1:
            near_array = lax.ppermute(near_array, "space", over_top)
        near.append([(near_array, 0, share)])
        if k < top - 1:
            far_array = lax.ppermute(near_array, "space", over_mid)
            far.append([(far_array, 0, share)])
        else:
            cut = share // 2
            upper = lax.ppermute(far_array[:cut], "space", over_top)
            lower = lax.ppermute(near_array[cut:], "space", over_mid)
            upper, lower, swapped = lax.optimization_barrier((upper, lower, swapped))
            far.append([(upper, 0, cut), (lower, 0, share - cut)])

    tiles, tile_ids, proposals = [], [], []

    def proposal_of(pieces):
        array, at, count = pieces[-1]
        return array[at + count :].reshape(cell_count)

    for k in range(top):
        at = (place + 4 * k) % tile_count
        for held, index in ((near[k], at), (far[k], at ^ 2)):
            sibling = [(forward(array), first_row, count) for array, first_row, count in held]
            for pieces, name in ((held, index), (sibling, index ^ 1)):
                tiles.append(pieces)
                tile_ids.append(name)
                proposals.append(proposal_of(pieces))
    tile_ids = jnp.stack(tile_ids)

    every = lax.dot_general(
        jnp.stack(proposals),
        own_blocks.reshape(block_count * obs_count, cell_count),
        (((1,), (1,)), ((), ())),
        preferred_element_type=jnp.float32,
    )
    named = tile_ids[:, None] == jnp.repeat(destination, obs_count)[None, :]
    predicted = jnp.sum(jnp.where(named, every, 0.0), axis=0, keepdims=True)
    misfit = soundings.reshape(1, -1).astype(jnp.float32) - predicted

    slots, counts = slots_of(destination, tile_ids, capacity)
    other_slots, other_counts = slots_of(other_destination, tile_ids, capacity)
    mine = [(own_blocks, side * share, share)]
    early = tile_count // 2
    own = block_products(
        slots, counts, mine, tiles, [(s, 0, share) for s in range(early)], capacity, jnp.float32
    )
    others = block_products(
        other_slots,
        other_counts,
        [(swapped, 0, share)],
        tiles,
        [(s, 0, share) for s in range(tile_count)],
        capacity,
        jnp.bfloat16,
    )
    received = lax.ppermute(others, "tm", over_step)
    own = block_products(
        slots,
        counts,
        mine,
        tiles,
        [(s, 0, share) for s in range(early, tile_count)],
        capacity,
        jnp.float32,
        own,
    )
    jac_scale = float(step_count * tile_count * block_count * obs_count) ** (-0.5)
    total = information_sums(own, received, misfit, jac_scale)

    half = total.shape[0] // 2
    last = place % 2
    mine = lax.dynamic_slice_in_dim(total, last * half, half, axis=0)
    sent = lax.dynamic_slice_in_dim(total, (1 - last) * half, half, axis=0)
    mine = mine + lax.ppermute(sent, "space", over_last)
    shift = 1
    while shift < step_count:
        pairs = [(i, i ^ shift) for i in range(step_count)]
        mine = mine + lax.ppermute(mine, "tm", pairs)
        shift *= 2
    shift = 2
    while shift < tile_count:
        pairs = [(i, i ^ shift) for i in range(tile_count)]
        mine = mine + lax.ppermute(mine, "space", pairs)
        shift *= 2
    back = lax.ppermute(mine, "space", over_last)
    packed = jnp.where(
        last == 0, jnp.concatenate([mine, back]), jnp.concatenate([back, mine])
    )
    factor_up, rhs = finish_factor(packed)
    return (
        proposal,
        predicted.reshape(1, block_count, obs_count),
        factor_up,
        rhs[0],
    )


def solution(mesh):
    return jax.shard_map(
        per_device,
        mesh=mesh,
        in_specs=(
            P("tm", "space"),
            P("tm", "space"),
            P("space"),
            P("tm", "space", None, None),
            P("tm", "space", None),
            P("tm", "space", None),
            P("space", None),
        ),
        out_specs=(P("tm", "space"), P("tm", "space", None), P(), P()),
        check_vma=False,
    )
```

```python
import jax
import jax.numpy as jnp
import numpy as np
from jax import lax
from jax.experimental import pallas as pl
from jax.experimental.pallas import tpu as pltpu
from jax.sharding import PartitionSpec as P

PATCH = 64
REACH = 8


BETA = 0.6
KEEP = 0.8
HIGHEST = lax.Precision.HIGHEST


def kernel_weights(reach):
    offsets = np.abs(np.arange(-reach, reach + 1)).astype(np.float32)
    profile = (1.0 + 2.0 * offsets / reach) * np.exp(-2.0 * offsets / reach)
    return [float(w) for w in profile / np.sqrt(np.sum(profile * profile))]


def make_proposal(flux, noise, prior_scale):
    edge = PATCH
    cells = flux.shape[1]
    width = REACH * edge
    weights = kernel_weights(REACH)
    devices = lax.axis_size("space")
    up = [(i, (i + 1) % devices) for i in range(devices - 1)]
    down = [(j, i) for i, j in up]
    before = lax.ppermute(noise[:, cells - width :], "space", up)
    after = lax.ppermute(noise[:, :width], "space", down)
    extended = jnp.concatenate([before, noise, after], axis=1).reshape(edge + 2 * REACH, edge)

    def kernel(extended_ref, flux_ref, scale_ref, out_ref):
        rows = jnp.zeros((edge, edge), jnp.float32)
        for position in range(2 * REACH + 1):
            rows = rows + weights[position] * extended_ref[position : position + edge, :]
        twice = jnp.concatenate([rows, rows], axis=1)
        smooth = jnp.zeros((edge, 2 * edge), jnp.float32)
        for position in range(2 * REACH + 1):
            shift = (REACH - position) % (2 * edge)
            rolled = pltpu.roll(twice, shift, 1) if shift else twice
            smooth = smooth + weights[position] * rolled
        out_ref[...] = KEEP * flux_ref[...] + BETA * scale_ref[...] * smooth[:, :edge]

    proposal = pl.pallas_call(
        kernel, out_shape=jax.ShapeDtypeStruct((edge, edge), jnp.float32)
    )(extended, flux.reshape(edge, edge), prior_scale.reshape(edge, edge))
    flat = proposal.reshape(1, cells)
    return flat, flat.astype(jnp.bfloat16)


def slots_of(destination, tile_ids, capacity):
    match = destination[None, :] == tile_ids[:, None]
    rank = jnp.cumsum(match.astype(jnp.int32), axis=1) - 1
    block = jnp.arange(destination.shape[0], dtype=jnp.int32)
    taken = match[:, None, :] & (rank[:, None, :] == jnp.arange(capacity)[None, :, None])
    slots = jnp.sum(jnp.where(taken, block[None, None, :], 0), axis=2)
    return slots.reshape(-1).astype(jnp.int32), jnp.sum(match, axis=1).astype(jnp.int32)


def block_products(slots, counts, sources, tiles, jobs, capacity, out_dtype, base=None):
    blocks, rows, _ = sources[0][0].shape
    rank = tiles[0][0][0].shape[1]
    widths = [width for _, _, width in sources]
    places = [sum(widths[:i]) for i in range(len(widths))]
    depth = max(high - low for _, low, high in jobs)
    arrays, copies = [], []
    for s, low, high in jobs:
        parts, at = [], 0
        for array, first, count in tiles[s]:
            begin, end = max(low, at), min(high, at + count)
            if begin < end:
                known = [i for i, other in enumerate(arrays) if other is array]
                if not known:
                    arrays.append(array)
                    known = [len(arrays) - 1]
                parts.append((known[0], first + begin - at, begin - low, end - begin))
            at += count
        copies.append(parts)
    most = max(len(parts) for parts in copies)

    def kernel(slots_ref, counts_ref, starts_ref, *rest):
        f_refs, rest = rest[: len(sources)], rest[len(sources) :]
        b_refs, rest = rest[: len(arrays)], rest[len(arrays) :]
        if base is not None:
            base_ref, rest = rest[0], rest[1:]
        (out_ref,) = rest
        begin = pl.multiple_of(starts_ref[0], 128)
        if base is not None and out_dtype == jnp.float32:
            out_ref[...] = base_ref[...]
        for n, (s, low, high) in enumerate(jobs):
            lhs = jnp.concatenate(
                [
                    f_refs[0][slots_ref[s * capacity + j], :, pl.ds(begin + low, high - low)]
                    for j in range(capacity)
                ],
                axis=0,
            )
            parts = [b_refs[i][first : first + count, :] for i, first, _, count in copies[n]]
            rhs = parts[0] if len(parts) == 1 else jnp.concatenate(parts, axis=0)
            product = jnp.dot(lhs, rhs, preferred_element_type=jnp.float32)
            for j in range(capacity):
                block = jnp.where(counts_ref[s] > j, slots_ref[s * capacity + j], blocks)
                at = pl.multiple_of(block * rows, rows)
                part = product[j * rows : (j + 1) * rows]
                if low > 0:
                    part = part + base_ref[pl.ds(at, rows), :]
                out_ref[pl.ds(at, rows), :] = part.astype(out_dtype)
        out_ref[blocks * rows :, :] = jnp.zeros((rows, rank), out_dtype)

    smem = pl.BlockSpec(memory_space=pltpu.SMEM)
    vmem = pl.BlockSpec(memory_space=pltpu.VMEM)
    hbm = pl.BlockSpec(memory_space=pl.ANY)
    extra = [] if base is None else [base]
    starts = jnp.stack([jnp.asarray(first, jnp.int32) for _, first, _ in sources])
    return pl.pallas_call(
        kernel,
        out_shape=jax.ShapeDtypeStruct(((blocks + 1) * rows, rank), out_dtype),
        in_specs=[smem] * 3 + [vmem] * (len(sources) + len(arrays) + len(extra)),
        out_specs=vmem,
        compiler_params=pltpu.CompilerParams(vmem_limit_bytes=60 * 2**20),
        cost_estimate=pl.CostEstimate(flops=1, bytes_accessed=1, transcendentals=0),
    )(slots, counts, starts, *[f for f, _, _ in sources], *arrays, *extra)


def arrival(array):
    def kernel(_, out_ref):
        out_ref[0] = 0

    return pl.pallas_call(
        kernel,
        out_shape=jax.ShapeDtypeStruct((1,), jnp.int32),
        in_specs=[pl.BlockSpec(memory_space=pl.ANY)],
        out_specs=pl.BlockSpec(memory_space=pltpu.SMEM),
        cost_estimate=pl.CostEstimate(flops=1, bytes_accessed=100 * 2**20, transcendentals=0),
    )(array)


def information_sums(own, received, misfit, scale):
    rows, rank = misfit.shape[1], own.shape[1]
    half = rank // 2
    packed = half + half // 2 + 16

    def kernel(own_ref, received_ref, misfit_ref, out_ref):
        jacobian = (own_ref[0:rows] + received_ref[0:rows].astype(jnp.float32)) * scale
        jacobian = jacobian.astype(jnp.bfloat16)
        gram = lax.dot_general(
            jacobian, jacobian, (((0,), (0,)), ((), ())), preferred_element_type=jnp.float32
        )
        out_ref[0:half, :] = gram[0:half, :]
        out_ref[half : half + half // 2, 0:half] = gram[half : half + half // 2, half:]
        out_ref[half : half + half // 2, half:] = gram[half + half // 2 :, half:]
        rest = misfit_ref[...]
        parts = []
        for _ in range(3):
            part = rest.astype(jnp.bfloat16)
            parts.append(part)
            rest = rest - part.astype(jnp.float32)
        lhs = jnp.concatenate(parts + [jnp.zeros((16 - 3, rows), jnp.bfloat16)], axis=0)
        projected = jnp.dot(lhs, jacobian, preferred_element_type=jnp.float32)
        total = projected[0:1] + projected[1:2] + projected[2:3]
        out_ref[half + half // 2 :, :] = jnp.broadcast_to(total, (16, rank))

    return pl.pallas_call(
        kernel,
        out_shape=jax.ShapeDtypeStruct((packed, rank), jnp.float32),
        compiler_params=pltpu.CompilerParams(vmem_limit_bytes=32 * 2**20),
    )(own, received, misfit)


def finish_factor(packed):
    rank = packed.shape[1]
    half = rank // 2
    quarter = half // 2
    wide = rank + 128
    strip = 64

    def kernel(in_ref, up_ref, rhs_ref, work, factor):
        top = in_ref[0:half, :]
        work[0:half, 0:rank] = top
        work[half:, 0:half] = top[:, half:].T
        work[half : half + quarter, half:rank] = in_ref[half : half + quarter, 0:half]
        work[half + quarter :, half:rank] = in_ref[half : half + quarter, half:]
        for k in range(0, rank, 128):
            row = lax.broadcasted_iota(jnp.int32, (128, 128), 0)
            col = lax.broadcasted_iota(jnp.int32, (128, 128), 1)
            work[k : k + 128, k : k + 128] += (row == col).astype(jnp.float32)
        column = in_ref[half + quarter : half + quarter + 8, :].T
        work[:, rank:] = jnp.broadcast_to(column[:, 0:1], (rank, 128))

        sub = lax.broadcasted_iota(jnp.int32, (8, wide), 0)
        for base in range(0, rank, strip):
            skip = base // 128 * 128
            width = wide - skip
            sub_w = sub[:, skip:]
            tiles = [work[base + 8 * i : base + 8 * i + 8, skip:] for i in range(strip // 8)]
            for p in range(strip // 8):
                at = base + 8 * p - skip
                r = [jnp.broadcast_to(tiles[p][j : j + 1, :], (8, width)) for j in range(8)]
                d = {}
                for j in range(8):
                    for m in range(j, 8):
                        d[j, m] = jnp.broadcast_to(r[j][:, at + m : at + m + 1], (8, 128))
                inv, e = [], {}
                for j in range(8):
                    inv.append(lax.rsqrt(d[j, j]))
                    for m in range(j + 1, 8):
                        e[j, m] = d[j, m] * inv[j]
                    for l in range(j + 1, 8):
                        for m in range(l, 8):
                            d[l, m] = d[l, m] - e[j, l] * e[j, m]
                lanes = lambda x: jnp.concatenate([x] * (width // 128), axis=1)
                u = []
                for j in range(8):
                    u.append(r[j] * lanes(inv[j]))
                    for l in range(j + 1, 8):
                        r[l] = r[l] - lanes(e[j, l]) * u[j]
                whole = jnp.zeros((8, width), jnp.float32)
                for j in range(8):
                    whole = jnp.where(sub_w == j, u[j], whole)
                factor[base + 8 * p : base + 8 * p + 8, skip:] = whole
                for i in range(p + 1, strip // 8):
                    a = [
                        jnp.broadcast_to(tiles[i][:, at + j : at + j + 1], (8, 128))
                        for j in range(8)
                    ]
                    tile = tiles[i]
                    for j in range(8):
                        m_j = a[j] * inv[j]
                        for l in range(j + 1, 8):
                            a[l] = a[l] - m_j * e[j, l]
                        tile = tile - lanes(m_j) * u[j]
                    tiles[i] = tile
            low = base + strip
            if low < rank:
                keep = low // 128 * 128
                left = factor[base:low, low:rank]
                right = factor[base:low, keep:]
                work[low:, keep:] -= lax.dot_general(
                    left,
                    right,
                    (((0,), (0,)), ((), ())),
                    precision=HIGHEST,
                    preferred_element_type=jnp.float32,
                )
        for k in range(0, rank, 128):
            for c in range(0, rank, 128):
                if c < k:
                    up_ref[k : k + 128, c : c + 128] = jnp.zeros((128, 128), jnp.float32)
                elif c > k:
                    up_ref[k : k + 128, c : c + 128] = factor[k : k + 128, c : c + 128]
                else:
                    row = lax.broadcasted_iota(jnp.int32, (128, 128), 0)
                    col = lax.broadcasted_iota(jnp.int32, (128, 128), 1)
                    up_ref[k : k + 128, c : c + 128] = jnp.where(
                        col >= row, factor[k : k + 128, c : c + 128], 0.0
                    )
            rhs_ref[:, k : k + 128] = factor[k : k + 128, rank:].T[0:8, :]

    return pl.pallas_call(
        kernel,
        out_shape=(
            jax.ShapeDtypeStruct((rank, rank), jnp.float32),
            jax.ShapeDtypeStruct((8, rank), jnp.float32),
        ),
        scratch_shapes=[
            pltpu.VMEM((rank, wide), jnp.float32),
            pltpu.VMEM((rank, wide), jnp.float32),
        ],
        compiler_params=pltpu.CompilerParams(vmem_limit_bytes=32 * 2**20),
    )(packed)


def per_device(flux, noise, prior_scale, footprints, soundings, targets, basis):
    tile_count = lax.axis_size("space")
    step_count = lax.axis_size("tm")
    _, block_count, obs_count, cell_count = footprints.shape
    rank = basis.shape[1]
    capacity = max(2, (2 * block_count + tile_count - 1) // tile_count)
    place = lax.axis_index("space")
    top = tile_count // 4
    side = lax.axis_index("tm") % 2
    share = cell_count // 2

    over_last = [(i, i ^ 1) for i in range(tile_count)]
    over_mid = [(i, i ^ 2) for i in range(tile_count)]
    over_top = [(i, (i - 4) % tile_count) for i in range(tile_count)]
    over_step = [(i, i ^ 1) for i in range(step_count)]

    destination = targets[0, :, 0]
    other_destination = lax.ppermute(destination, "tm", over_step)

    own_blocks = footprints[0]
    begin = (1 - side) * share
    to_send = lax.dynamic_slice_in_dim(own_blocks, begin, share, axis=2)
    to_send, other_destination = lax.optimization_barrier((to_send, other_destination))
    swapped = lax.ppermute(to_send, "tm", over_step)
    zero = arrival(swapped)[0]

    noise, _ = lax.optimization_barrier((noise, to_send))
    proposal, rounded = make_proposal(flux, noise, prior_scale)
    own_half = lax.dynamic_slice_in_dim(basis, side * share, share, axis=0)
    rounded = rounded.reshape(-1, rank)

    def forward(x):
        return lax.ppermute(x, "space", over_last)

    def both(way):
        return jnp.concatenate(
            [lax.ppermute(x, "space", way) for x in (own_half, rounded)], axis=0
        )

    near = [[(own_half, 0, share), (rounded, 0, 0)]]
    near_array, far_array = both(over_top), both(over_mid)
    far = [[(far_array, 0, share)]]
    for k in range(1, top):
        if k > 1:
            near_array = lax.ppermute(near_array, "space", over_top)
        near.append([(near_array, 0, share)])
        if k < top - 1:
            far_array = lax.ppermute(near_array, "space", over_mid)
            far.append([(far_array, 0, share)])
        else:
            cut = share // 2
            upper = lax.ppermute(far_array[:cut], "space", over_top)
            lower = lax.ppermute(near_array[cut:], "space", over_mid)
            far.append([(upper, 0, cut), (lower, 0, share - cut)])

    tiles, tile_ids, proposals = [], [], []

    def add_tile(pieces, index):
        sibling = [(forward(array), first_row, count) for array, first_row, count in pieces]
        for parts, name in ((pieces, index), (sibling, index ^ 1)):
            tiles.append(parts)
            tile_ids.append(name)
            array, at, count = parts[-1]
            proposals.append(array[at + count :].reshape(cell_count))

    for k in range(top):
        add_tile(near[k], (place + 4 * k) % tile_count)
        if k < top - 1:
            add_tile(far[k], ((place + 4 * k) % tile_count) ^ 2)
    early = len(tiles) - 4
    slots, counts = slots_of(destination, jnp.stack(tile_ids), capacity)
    mine = [(own_blocks, side * share, share)]
    own = block_products(
        slots, counts, mine, tiles, [(s, 0, share) for s in range(early)], capacity, jnp.float32
    )
    upper, lower, own, zero = lax.optimization_barrier((upper, lower, own, zero))
    far[-1] = [(upper, 0, cut), (lower, 0, share - cut)]
    add_tile(far[-1], ((place + 4 * (top - 1)) % tile_count) ^ 2)
    tile_ids = jnp.stack(tile_ids)

    every = lax.dot_general(
        jnp.stack(proposals),
        own_blocks.reshape(block_count * obs_count, cell_count),
        (((1,), (1,)), ((), ())),
        preferred_element_type=jnp.float32,
    )
    named = tile_ids[:, None] == jnp.repeat(destination, obs_count)[None, :]
    predicted = jnp.sum(jnp.where(named, every, 0.0), axis=0, keepdims=True)
    misfit = soundings.reshape(1, -1).astype(jnp.float32) - predicted

    slots, counts = slots_of(destination, tile_ids, capacity)
    other_slots, other_counts = slots_of(other_destination, tile_ids, capacity)
    others = block_products(
        other_slots,
        other_counts,
        [(swapped, zero, share)],
        tiles,
        [(s, 0, share) for s in range(tile_count)],
        capacity,
        jnp.bfloat16,
    )
    received = lax.ppermute(others, "tm", over_step)
    own = block_products(
        slots,
        counts,
        mine,
        tiles,
        [(s, 0, share) for s in range(early, tile_count)],
        capacity,
        jnp.float32,
        own,
    )
    jac_scale = float(step_count * tile_count * block_count * obs_count) ** (-0.5)
    total = information_sums(own, received, misfit, jac_scale)

    half = total.shape[0] // 2
    last = place % 2
    mine = lax.dynamic_slice_in_dim(total, last * half, half, axis=0)
    sent = lax.dynamic_slice_in_dim(total, (1 - last) * half, half, axis=0)
    mine = mine + lax.ppermute(sent, "space", over_last)
    shift = 1
    while shift < step_count:
        pairs = [(i, i ^ shift) for i in range(step_count)]
        mine = mine + lax.ppermute(mine, "tm", pairs)
        shift *= 2
    shift = 2
    while shift < tile_count:
        pairs = [(i, i ^ shift) for i in range(tile_count)]
        mine = mine + lax.ppermute(mine, "space", pairs)
        shift *= 2
    back = lax.ppermute(mine, "space", over_last)
    packed = jnp.where(
        last == 0, jnp.concatenate([mine, back]), jnp.concatenate([back, mine])
    )
    factor_up, rhs = finish_factor(packed)
    return (
        proposal,
        predicted.reshape(1, block_count, obs_count),
        factor_up,
        rhs[0],
    )


def solution(mesh):
    return jax.shard_map(
        per_device,
        mesh=mesh,
        in_specs=(
            P("tm", "space"),
            P("tm", "space"),
            P("space"),
            P("tm", "space", None, None),
            P("tm", "space", None),
            P("tm", "space", None),
            P("space", None),
        ),
        out_specs=(P("tm", "space"), P("tm", "space", None), P(), P()),
        check_vma=False,
    )
```

```python
import jax
import jax.numpy as jnp
import numpy as np
from jax import lax
from jax.experimental import pallas as pl
from jax.experimental.pallas import tpu as pltpu
from jax.sharding import PartitionSpec as P

PATCH = 64
REACH = 8


BETA = 0.6
KEEP = 0.8
HIGHEST = lax.Precision.HIGHEST


def kernel_weights(reach):
    offsets = np.abs(np.arange(-reach, reach + 1)).astype(np.float32)
    profile = (1.0 + 2.0 * offsets / reach) * np.exp(-2.0 * offsets / reach)
    return [float(w) for w in profile / np.sqrt(np.sum(profile * profile))]


def make_proposal(flux, noise, prior_scale):
    edge = PATCH
    cells = flux.shape[1]
    width = REACH * edge
    weights = kernel_weights(REACH)
    devices = lax.axis_size("space")
    up = [(i, (i + 1) % devices) for i in range(devices - 1)]
    down = [(j, i) for i, j in up]
    before = lax.ppermute(noise[:, cells - width :], "space", up)
    after = lax.ppermute(noise[:, :width], "space", down)
    extended = jnp.concatenate([before, noise, after], axis=1).reshape(edge + 2 * REACH, edge)

    def kernel(extended_ref, flux_ref, scale_ref, out_ref):
        rows = jnp.zeros((edge, edge), jnp.float32)
        for position in range(2 * REACH + 1):
            rows = rows + weights[position] * extended_ref[position : position + edge, :]
        twice = jnp.concatenate([rows, rows], axis=1)
        smooth = jnp.zeros((edge, 2 * edge), jnp.float32)
        for position in range(2 * REACH + 1):
            shift = (REACH - position) % (2 * edge)
            rolled = pltpu.roll(twice, shift, 1) if shift else twice
            smooth = smooth + weights[position] * rolled
        out_ref[...] = KEEP * flux_ref[...] + BETA * scale_ref[...] * smooth[:, :edge]

    proposal = pl.pallas_call(
        kernel, out_shape=jax.ShapeDtypeStruct((edge, edge), jnp.float32)
    )(extended, flux.reshape(edge, edge), prior_scale.reshape(edge, edge))
    flat = proposal.reshape(1, cells)
    return flat, flat.astype(jnp.bfloat16)


def slots_of(destination, tile_ids, capacity):
    match = destination[None, :] == tile_ids[:, None]
    rank = jnp.cumsum(match.astype(jnp.int32), axis=1) - 1
    block = jnp.arange(destination.shape[0], dtype=jnp.int32)
    taken = match[:, None, :] & (rank[:, None, :] == jnp.arange(capacity)[None, :, None])
    slots = jnp.sum(jnp.where(taken, block[None, None, :], 0), axis=2)
    return slots.reshape(-1).astype(jnp.int32), jnp.sum(match, axis=1).astype(jnp.int32)


def block_products(slots, counts, sources, tiles, jobs, capacity, out_dtype, base=None):
    blocks, rows, _ = sources[0][0].shape
    rank = tiles[0][0][0].shape[1]
    widths = [width for _, _, width in sources]
    places = [sum(widths[:i]) for i in range(len(widths))]
    depth = max(high - low for _, low, high in jobs)
    arrays, copies = [], []
    for s, low, high in jobs:
        parts, at = [], 0
        for array, first, count in tiles[s]:
            begin, end = max(low, at), min(high, at + count)
            if begin < end:
                known = [i for i, other in enumerate(arrays) if other is array]
                if not known:
                    arrays.append(array)
                    known = [len(arrays) - 1]
                parts.append((known[0], first + begin - at, begin - low, end - begin))
            at += count
        copies.append(parts)
    most = max(len(parts) for parts in copies)

    def kernel(slots_ref, counts_ref, starts_ref, *rest):
        f_refs, rest = rest[: len(sources)], rest[len(sources) :]
        b_refs, rest = rest[: len(arrays)], rest[len(arrays) :]
        if base is not None:
            base_ref, rest = rest[0], rest[1:]
        (out_ref,) = rest
        begin = pl.multiple_of(starts_ref[0], 128)
        if base is not None and out_dtype == jnp.float32:
            out_ref[...] = base_ref[...]
        for n, (s, low, high) in enumerate(jobs):
            lhs = jnp.concatenate(
                [
                    f_refs[0][slots_ref[s * capacity + j], :, pl.ds(begin + low, high - low)]
                    for j in range(capacity)
                ],
                axis=0,
            )
            parts = [b_refs[i][first : first + count, :] for i, first, _, count in copies[n]]
            rhs = parts[0] if len(parts) == 1 else jnp.concatenate(parts, axis=0)
            product = jnp.dot(lhs, rhs, preferred_element_type=jnp.float32)
            for j in range(capacity):
                block = jnp.where(counts_ref[s] > j, slots_ref[s * capacity + j], blocks)
                at = pl.multiple_of(block * rows, rows)
                part = product[j * rows : (j + 1) * rows]
                if low > 0:
                    part = part + base_ref[pl.ds(at, rows), :]
                out_ref[pl.ds(at, rows), :] = part.astype(out_dtype)
        out_ref[blocks * rows :, :] = jnp.zeros((rows, rank), out_dtype)

    smem = pl.BlockSpec(memory_space=pltpu.SMEM)
    vmem = pl.BlockSpec(memory_space=pltpu.VMEM)
    hbm = pl.BlockSpec(memory_space=pl.ANY)
    extra = [] if base is None else [base]
    starts = jnp.stack([jnp.asarray(first, jnp.int32) for _, first, _ in sources])
    return pl.pallas_call(
        kernel,
        out_shape=jax.ShapeDtypeStruct(((blocks + 1) * rows, rank), out_dtype),
        in_specs=[smem] * 3 + [vmem] * (len(sources) + len(arrays) + len(extra)),
        out_specs=vmem,
        compiler_params=pltpu.CompilerParams(vmem_limit_bytes=60 * 2**20),
        cost_estimate=pl.CostEstimate(flops=1, bytes_accessed=1, transcendentals=0),
    )(slots, counts, starts, *[f for f, _, _ in sources], *arrays, *extra)


def arrival(array):
    def kernel(_, out_ref):
        out_ref[0] = 0

    return pl.pallas_call(
        kernel,
        out_shape=jax.ShapeDtypeStruct((1,), jnp.int32),
        in_specs=[pl.BlockSpec(memory_space=pl.ANY)],
        out_specs=pl.BlockSpec(memory_space=pltpu.SMEM),
        cost_estimate=pl.CostEstimate(flops=1, bytes_accessed=100 * 2**20, transcendentals=0),
    )(array)


def information_sums(own, received, misfit, scale):
    rows, rank = misfit.shape[1], own.shape[1]
    half, part = rank // 2, rank // 4
    blocks = 2 * part + part // 2

    def kernel(own_ref, received_ref, misfit_ref, out_ref):
        jacobian = (own_ref[0:rows] + received_ref[0:rows].astype(jnp.float32)) * scale
        jacobian = jacobian.astype(jnp.bfloat16)
        gram = lax.dot_general(
            jacobian, jacobian, (((0,), (0,)), ((), ())), preferred_element_type=jnp.float32
        )
        out_ref[0:part, :] = gram[0:part, :]
        out_ref[part:half, part:] = gram[part:half, part:]
        out_ref[part:half, 0:part] = gram[half + part :, half + part :]
        out_ref[half:blocks, 0:half] = gram[half : half + part // 2, half:]
        out_ref[half:blocks, half:] = gram[half + part // 2 : half + part, half:]
        rest = misfit_ref[...]
        parts = []
        for _ in range(3):
            piece = rest.astype(jnp.bfloat16)
            parts.append(piece)
            rest = rest - piece.astype(jnp.float32)
        lhs = jnp.concatenate(parts + [jnp.zeros((16 - 3, rows), jnp.bfloat16)], axis=0)
        projected = jnp.dot(lhs, jacobian, preferred_element_type=jnp.float32)
        total = projected[0:1] + projected[1:2] + projected[2:3]
        out_ref[blocks:, :] = jnp.broadcast_to(total, (16, rank))

    return pl.pallas_call(
        kernel,
        out_shape=jax.ShapeDtypeStruct((blocks + 16, rank), jnp.float32),
        compiler_params=pltpu.CompilerParams(vmem_limit_bytes=32 * 2**20),
    )(own, received, misfit)


def finish_factor(mine, back, last):
    rank = mine.shape[1]
    half, strip = rank // 2, rank // 4
    wide = rank + 128
    blocks = 2 * strip + strip // 2

    def kernel(last_ref, mine_ref, back_ref, up_ref, rhs_ref, sums, work, factor):
        own_half = mine_ref.shape[0]

        @pl.when(last_ref[0] == 0)
        def _():
            sums[0:own_half, :] = mine_ref[...]
            sums[own_half:, :] = back_ref[...]

        @pl.when(last_ref[0] != 0)
        def _():
            sums[0:own_half, :] = back_ref[...]
            sums[own_half:, :] = mine_ref[...]

        work[0:strip, 0:rank] = sums[0:strip, :]
        work[strip:half, 0:rank] = sums[strip:half, :]
        work[half : half + strip // 2, half:rank] = sums[half:blocks, 0:half]
        work[half + strip // 2 : half + strip, half:rank] = sums[half:blocks, half:]
        corner = sums[strip:half, 0:half]
        work[half + strip :, half:rank] = jnp.concatenate(
            [jnp.zeros((strip, strip), jnp.float32), corner[:, 0:strip]], axis=1
        )
        for k in range(0, rank, 128):
            row = lax.broadcasted_iota(jnp.int32, (128, 128), 0)
            col = lax.broadcasted_iota(jnp.int32, (128, 128), 1)
            work[k : k + 128, k : k + 128] += (row == col).astype(jnp.float32)
        column = sums[blocks : blocks + 8, :].T
        work[:, rank:] = jnp.broadcast_to(column[:, 0:1], (rank, 128))

        sub = lax.broadcasted_iota(jnp.int32, (8, wide), 0)
        for base in range(0, rank, strip):
            skip = base // 128 * 128
            width = wide - skip
            sub_w = sub[:, skip:]
            tiles = [work[base + 8 * i : base + 8 * i + 8, skip:] for i in range(strip // 8)]
            for p in range(strip // 8):
                at = base + 8 * p - skip
                r = [jnp.broadcast_to(tiles[p][j : j + 1, :], (8, width)) for j in range(8)]
                d = {}
                for j in range(8):
                    for m in range(j, 8):
                        d[j, m] = jnp.broadcast_to(r[j][:, at + m : at + m + 1], (8, 128))
                inv, e = [], {}
                for j in range(8):
                    inv.append(lax.rsqrt(d[j, j]))
                    for m in range(j + 1, 8):
                        e[j, m] = d[j, m] * inv[j]
                    for l in range(j + 1, 8):
                        for m in range(l, 8):
                            d[l, m] = d[l, m] - e[j, l] * e[j, m]
                lanes = lambda x: jnp.concatenate([x] * (width // 128), axis=1)
                u = []
                for j in range(8):
                    u.append(r[j] * lanes(inv[j]))
                    for l in range(j + 1, 8):
                        r[l] = r[l] - lanes(e[j, l]) * u[j]
                whole = jnp.zeros((8, width), jnp.float32)
                for j in range(8):
                    whole = jnp.where(sub_w == j, u[j], whole)
                factor[base + 8 * p : base + 8 * p + 8, skip:] = whole
                for i in range(p + 1, strip // 8):
                    a = [
                        jnp.broadcast_to(tiles[i][:, at + j : at + j + 1], (8, 128))
                        for j in range(8)
                    ]
                    tile = tiles[i]
                    for j in range(8):
                        m_j = a[j] * inv[j]
                        for l in range(j + 1, 8):
                            a[l] = a[l] - m_j * e[j, l]
                        tile = tile - lanes(m_j) * u[j]
                    tiles[i] = tile
            low = base + strip
            if low < rank:
                keep = low // 128 * 128
                left = factor[base:low, low:rank]
                right = factor[base:low, keep:]
                work[low:, keep:] -= lax.dot_general(
                    left,
                    right,
                    (((0,), (0,)), ((), ())),
                    precision=HIGHEST,
                    preferred_element_type=jnp.float32,
                )
        for k in range(0, rank, 128):
            for c in range(0, rank, 128):
                if c < k:
                    up_ref[k : k + 128, c : c + 128] = jnp.zeros((128, 128), jnp.float32)
                elif c > k:
                    up_ref[k : k + 128, c : c + 128] = factor[k : k + 128, c : c + 128]
                else:
                    row = lax.broadcasted_iota(jnp.int32, (128, 128), 0)
                    col = lax.broadcasted_iota(jnp.int32, (128, 128), 1)
                    up_ref[k : k + 128, c : c + 128] = jnp.where(
                        col >= row, factor[k : k + 128, c : c + 128], 0.0
                    )
            rhs_ref[:, k : k + 128] = factor[k : k + 128, rank:].T[0:1, :]

    return pl.pallas_call(
        kernel,
        out_shape=(
            jax.ShapeDtypeStruct((rank, rank), jnp.float32),
            jax.ShapeDtypeStruct((1, rank), jnp.float32),
        ),
        in_specs=[pl.BlockSpec(memory_space=pltpu.SMEM)]
        + [pl.BlockSpec(memory_space=pltpu.VMEM)] * 2,
        scratch_shapes=[
            pltpu.VMEM((blocks + 16, rank), jnp.float32),
            pltpu.VMEM((rank, wide), jnp.float32),
            pltpu.VMEM((rank, wide), jnp.float32),
        ],
        compiler_params=pltpu.CompilerParams(vmem_limit_bytes=32 * 2**20),
    )(last.astype(jnp.int32).reshape(1), mine, back)


def per_device(flux, noise, prior_scale, footprints, soundings, targets, basis):
    tile_count = lax.axis_size("space")
    step_count = lax.axis_size("tm")
    _, block_count, obs_count, cell_count = footprints.shape
    rank = basis.shape[1]
    capacity = max(2, (2 * block_count + tile_count - 1) // tile_count)
    place = lax.axis_index("space")
    top = tile_count // 4
    side = lax.axis_index("tm") % 2
    share = cell_count // 2

    over_last = [(i, i ^ 1) for i in range(tile_count)]
    over_mid = [(i, i ^ 2) for i in range(tile_count)]
    over_top = [(i, (i - 4) % tile_count) for i in range(tile_count)]
    over_step = [(i, i ^ 1) for i in range(step_count)]

    destination = targets[0, :, 0]
    other_destination = lax.ppermute(destination, "tm", over_step)

    own_blocks = footprints[0]
    begin = (1 - side) * share
    to_send = lax.dynamic_slice_in_dim(own_blocks, begin, share, axis=2)
    to_send, other_destination = lax.optimization_barrier((to_send, other_destination))
    swapped = lax.ppermute(to_send, "tm", over_step)
    zero = arrival(swapped)[0]

    noise, _ = lax.optimization_barrier((noise, to_send))
    proposal, rounded = make_proposal(flux, noise, prior_scale)
    own_half = lax.dynamic_slice_in_dim(basis, side * share, share, axis=0)
    rounded = rounded.reshape(-1, rank)

    def forward(x):
        return lax.ppermute(x, "space", over_last)

    def both(way):
        return jnp.concatenate(
            [lax.ppermute(x, "space", way) for x in (own_half, rounded)], axis=0
        )

    near = [[(own_half, 0, share), (rounded, 0, 0)]]
    near_array, far_array = both(over_top), both(over_mid)
    far = [[(far_array, 0, share)]]
    for k in range(1, top):
        if k > 1:
            near_array = lax.ppermute(near_array, "space", over_top)
        near.append([(near_array, 0, share)])
        if k < top - 1:
            far_array = lax.ppermute(near_array, "space", over_mid)
            far.append([(far_array, 0, share)])
        else:
            cut = share // 2
            upper = lax.ppermute(far_array[:cut], "space", over_top)
            lower = lax.ppermute(near_array[cut:], "space", over_mid)
            far.append([(upper, 0, cut), (lower, 0, share - cut)])

    tiles, tile_ids, proposals = [], [], []

    def add_tile(pieces, index):
        sibling = [(forward(array), first_row, count) for array, first_row, count in pieces]
        for parts, name in ((pieces, index), (sibling, index ^ 1)):
            tiles.append(parts)
            tile_ids.append(name)
            array, at, count = parts[-1]
            proposals.append(array[at + count :].reshape(cell_count))

    for k in range(top):
        add_tile(near[k], (place + 4 * k) % tile_count)
        if k < top - 1:
            add_tile(far[k], ((place + 4 * k) % tile_count) ^ 2)
    early = len(tiles) - 4
    slots, counts = slots_of(destination, jnp.stack(tile_ids), capacity)
    mine = [(own_blocks, side * share, share)]
    own = block_products(
        slots, counts, mine, tiles, [(s, 0, share) for s in range(early)], capacity, jnp.float32
    )
    upper, lower, own, zero = lax.optimization_barrier((upper, lower, own, zero))
    far[-1] = [(upper, 0, cut), (lower, 0, share - cut)]
    add_tile(far[-1], ((place + 4 * (top - 1)) % tile_count) ^ 2)
    tile_ids = jnp.stack(tile_ids)

    every = lax.dot_general(
        jnp.stack(proposals),
        own_blocks.reshape(block_count * obs_count, cell_count),
        (((1,), (1,)), ((), ())),
        preferred_element_type=jnp.float32,
    )
    named = tile_ids[:, None] == jnp.repeat(destination, obs_count)[None, :]
    predicted = jnp.sum(jnp.where(named, every, 0.0), axis=0, keepdims=True)
    misfit = soundings.reshape(1, -1).astype(jnp.float32) - predicted

    slots, counts = slots_of(destination, tile_ids, capacity)
    other_slots, other_counts = slots_of(other_destination, tile_ids, capacity)
    others = block_products(
        other_slots,
        other_counts,
        [(swapped, zero, share)],
        tiles,
        [(s, 0, share) for s in range(tile_count)],
        capacity,
        jnp.bfloat16,
    )
    received = lax.ppermute(others, "tm", over_step)
    own = block_products(
        slots,
        counts,
        mine,
        tiles,
        [(s, 0, share) for s in range(early, tile_count)],
        capacity,
        jnp.float32,
        own,
    )
    jac_scale = float(step_count * tile_count * block_count * obs_count) ** (-0.5)
    total = information_sums(own, received, misfit, jac_scale)

    half = total.shape[0] // 2
    last = place % 2
    mine = lax.dynamic_slice_in_dim(total, last * half, half, axis=0)
    sent = lax.dynamic_slice_in_dim(total, (1 - last) * half, half, axis=0)
    mine = mine + lax.ppermute(sent, "space", over_last)
    shift = 1
    while shift < step_count:
        pairs = [(i, i ^ shift) for i in range(step_count)]
        mine = mine + lax.ppermute(mine, "tm", pairs)
        shift *= 2
    shift = 2
    while shift < tile_count:
        pairs = [(i, i ^ shift) for i in range(tile_count)]
        mine = mine + lax.ppermute(mine, "space", pairs)
        shift *= 2
    back = lax.ppermute(mine, "space", over_last)
    factor_up, rhs = finish_factor(mine, back, last)
    return (
        proposal,
        predicted.reshape(1, block_count, obs_count),
        factor_up,
        rhs.reshape(rank),
    )


def solution(mesh):
    return jax.shard_map(
        per_device,
        mesh=mesh,
        in_specs=(
            P("tm", "space"),
            P("tm", "space"),
            P("space"),
            P("tm", "space", None, None),
            P("tm", "space", None),
            P("tm", "space", None),
            P("space", None),
        ),
        out_specs=(P("tm", "space"), P("tm", "space", None), P(), P()),
        check_vma=False,
    )
```
